32 devices in a mesh: frag: 2 (over x), aux: 2 (over core), ao: 8 (over z, y).
Axes of the slice: x: 2, y: 2, z: 4, core: 2. Of those that a mesh axis runs over, the one named last changes fastest.
Arguments:
- factors: bfloat16 [4, 24576, 1024], P(None, ('frag', 'aux'), 'ao'), parts along dimension 1, may hold values from -0.41992188 to 0.41992188
- pairs: int32 [16, 2], P('frag'), parts along dimension 0, may hold values from 0 to 7, as said below
- owners: int32 [16, 2], P('frag'), parts along dimension 0, may hold values from 0 to 7, all different within a row; in each aligned block of 8 rows (0 to 7, 8 to 15, ...) at most 4 rows name the same one
Outputs:
- ktiles: float32 [64, 128, 128], P(('frag', 'ao'), 'aux'), parts along dimension 0
The draws below stay inside these ranges and needn't reach their ends.
There are 2 independent parts, one for each index of `frag`. The reference program is written for one: setup_inputs(seed, part) draws one part's arguments, and reference() takes and returns one part's arrays. A program takes and returns all parts, laid end to end along the dimension named above; each array names one. Nothing has to cross between parts.
Inputs may be any that keep to these rules, and one draw needn't show every extreme that they name: `pairs`: the two blocks of a pair differ; a pair may repeat. The two owners of a pair differ; no ao index owns more than 4 entries, a bound that some block reaches.
All inputs are finite; a program needn't handle non-finite values.
Results may differ from the reference program's by a relative error of at most 0.0003.
Values may be sent and summed in bfloat16 or wider, within the bound.
A program may use at most 128 MiB of HBM per device.

```python
import math
import jax
import jax.numpy as jnp
import numpy as np
from jax import lax

BLK = 128
OCC = 4
NAUX = 12288
NBLOCKS = 8
NAO = 1024
PAIRS = 8
CAP = 4
N_AO = 8


def draw_pairs(key, part):
    key = jax.random.fold_in(key, 11)
    first_key, step_key = jax.random.split(key)
    first = jax.random.randint(first_key, (PAIRS,), 0, NBLOCKS)
    step = jax.random.randint(step_key, (PAIRS,), 1, NBLOCKS)
    second = (first + step) % NBLOCKS
    return jnp.stack([first, second], axis=1).astype(jnp.int32)


def block_levels(stream_key, extent, pieces, least, largest):
    factor_of = 1.0
    for dim, shards_of in pieces:
        heights = jax.random.uniform(jax.random.fold_in(jax.random.fold_in(stream_key, 6), dim), (shards_of,), jnp.float32, least / len(pieces), largest / len(pieces))
        factor_of = factor_of * jnp.repeat(jnp.exp(heights), extent[dim] // shards_of).reshape((-1,) + (1,) * (len(extent) - 1 - dim))
    return factor_of


def shared_out(key, own, number, rows, amount, top, reach, skew):
    order = jax.random.permutation(key, amount)
    packed, common = shares(amount, rows * top, reach, skew, True), shares(amount, rows * top, reach, skew, False)
    places = jnp.arange(amount)

    def named(tallies, turn):
        used = int((tallies > 0).sum())
        fixed = max(1, used // 4)
        passed = fixed + (places - fixed + turn * (used - fixed)) % max(1, amount - fixed)
        return jnp.zeros((amount,), jnp.int32).at[order[jnp.where(places < fixed, places, passed)]].set(jnp.asarray(tallies, jnp.int32))

    tallies = jnp.where(number % 4 == 0, named(packed, number // 4), named(common, number - number // 4 - 1))
    mixed = jax.random.permutation(jax.random.fold_in(own, 3), amount)
    donor, sink = mixed[0:amount // 2 * 2:2], mixed[1:amount // 2 * 2:2]
    room = jnp.minimum(tallies[donor] - 1, reach - tallies[sink]) // 2
    room = jnp.where((donor == order[0]) | (sink == order[0]) | (tallies[sink] == 0), 0, jnp.maximum(room, 0))
    passed = jax.random.randint(jax.random.fold_in(own, 4), (amount // 2,), 0, 1 << 20) % (room + 1)
    tallies = tallies.at[donor].add(-passed).at[sink].add(passed)
    members = jnp.searchsorted(jnp.cumsum(tallies), jnp.arange(rows * top), side="right").astype(jnp.int32)
    table = members.reshape(top, rows).T
    table = table[jax.random.permutation(jax.random.fold_in(own, 1), rows)]
    turn = jax.random.randint(jax.random.fold_in(own, 2), (rows, 1), 0, top)
    return jnp.take_along_axis(table, (jnp.arange(top)[None, :] + turn) % top, axis=1)


def shares(amount, total, most, skew, full):
    portions = [(1 << 20) // math.isqrt(grade ** skew) + 1 for grade in range(1, amount + 1)]
    largest = most if full else min(most, max(-(-total // amount), total * portions[0] // sum(portions)))
    least = 1 if total - largest >= amount - 1 else 0
    given, rest = [largest] + [least] * (amount - 1), total - largest - least * (amount - 1)
    while rest > 0:
        candidates = [i for i in range(1, amount) if given[i] < largest] or [i for i in range(1, amount) if given[i] < most]
        pool, budget = sum([portions[i] for i in candidates]), rest
        for i in candidates:
            extra = min(most - given[i], max(1, budget * portions[i] // pool), rest)
            given[i] = given[i] + extra
            rest = rest - extra
    return np.array(given)


def bell_draw(key, dims, scale, limit, pieces=(), held_as=jnp.bfloat16):
    drawn = scale * jax.random.normal(key, dims, jnp.float32)
    if pieces:
        drawn = drawn * block_levels(key, dims, pieces, -0.22, 0.18)
    return jnp.clip(drawn, -limit, limit).astype(held_as)


def setup_inputs(seed: int = 0, part: int = 0) -> dict:
    seeds = jax.random.split(jax.random.key(seed), 4)
    own_keys = jax.random.split(jax.random.fold_in(seeds[3], part), 4)
    factors = bell_draw(own_keys[0], (OCC, NAUX, NAO), 0.07, 0.41992188, ((1, 2), (2, 8)))
    pairs = draw_pairs(jax.random.fold_in(jax.random.fold_in(seeds[3], part), 71), part)
    owners_keys = jax.random.split(jax.random.fold_in(own_keys[2], 1), PAIRS // PAIRS)
    owners_turns = jax.random.permutation(jax.random.fold_in(own_keys[2], 3), PAIRS // PAIRS)
    owners = jax.vmap(lambda own, number: shared_out(jax.random.fold_in(own_keys[2], 2), own, number, PAIRS, N_AO, 2, CAP, 2))(owners_keys, owners_turns).reshape((PAIRS, 2))
    return dict(factors=factors, pairs=pairs, owners=owners)


def slot_table(pairs, owners, n_owner, capacity):
    count = pairs.shape[0]
    owner_flat = jnp.concatenate([owners[:, 0], owners[:, 1]]).astype(jnp.int32)
    hits = (owner_flat[:, None] == jnp.arange(n_owner, dtype=jnp.int32)[None, :]).astype(jnp.int32)
    ranks = jnp.sum(hits * (jnp.cumsum(hits, axis=0) - 1), axis=1)
    slot_of = owner_flat * capacity + ranks
    match = (slot_of[None, :] == jnp.arange(n_owner * capacity, dtype=jnp.int32)[:, None]).astype(jnp.int32)
    entry = jnp.sum(match * jnp.arange(2 * count, dtype=jnp.int32)[None, :], axis=1)
    filled = jnp.sum(match, axis=1)
    return entry, filled


def reference(factors, pairs, owners):
    depth = factors.shape[0] * factors.shape[1]
    flat = factors.reshape(depth, factors.shape[2])

    def one_pair(pair):
        left = lax.dynamic_slice_in_dim(flat, (pair[0] * BLK).astype(jnp.int32), BLK, 1)
        right = lax.dynamic_slice_in_dim(flat, (pair[1] * BLK).astype(jnp.int32), BLK, 1)
        return jnp.dot(left.T, right, preferred_element_type=jnp.float32)

    tiles = lax.map(one_pair, pairs)
    entries = jnp.concatenate([tiles, jnp.swapaxes(tiles, 1, 2)], axis=0)
    entry, filled = slot_table(pairs, owners, N_AO, CAP)
    return jnp.take(entries, entry, axis=0) * filled[:, None, None].astype(jnp.float32)
```

```python
import functools

import jax
import jax.numpy as jnp
from jax import lax
from jax.experimental import pallas as pl
from jax.experimental.pallas import tpu as pltpu
from jax.sharding import PartitionSpec as P

CAP = 4
MESH = pl.DeviceIdType.MESH


def kernel(n_ao, n_aux, occupied, pairs_ref, owners_ref, factors_ref, out_ref, *scratch):
    bufs = scratch[:occupied]
    acc, from_core, from_ao, piece, tiles = scratch[occupied : occupied + 5]
    own_sem, send_sem, recv_sem, core_sem, part_sem, spread_sem, pass_sem = scratch[occupied + 5 :]
    me = lax.axis_index("ao")
    core = lax.axis_index("aux")
    other = 1 - core
    rows, block = bufs[0].shape[1:]
    count = pairs_ref.shape[0]
    half = out_ref.shape[1]
    share = acc.shape[0] // n_aux
    size = share // n_ao
    pieces = block // size

    def peer(k):
        return lax.rem(me + k, n_ao)

    def source(k):
        return lax.rem(me + (n_ao - k), n_ao)

    barrier = pltpu.get_barrier_semaphore()
    for k in range(1, n_ao):
        pl.semaphore_signal(barrier, inc=1, device_id={"ao": peer(k)}, device_id_type=MESH)
    pl.semaphore_signal(barrier, inc=1, device_id={"aux": other}, device_id_type=MESH)
    own = []
    for o in range(occupied):
        copy = pltpu.make_async_copy(
            factors_ref.at[o, pl.ds(pl.multiple_of(me * rows, 16), rows)], bufs[o].at[me], own_sem.at[o]
        )
        copy.start()
        own.append(copy)
    pl.semaphore_wait(barrier, n_ao)

    def move(o, k):
        return pltpu.make_async_remote_copy(
            src_ref=factors_ref.at[o, pl.ds(pl.multiple_of(peer(k) * rows, 16), rows)],
            dst_ref=bufs[o].at[me],
            send_sem=send_sem.at[o, k],
            recv_sem=recv_sem.at[o, k],
            device_id={"ao": peer(k)},
            device_id_type=MESH,
        )

    order = sorted(range(1, n_ao), key=lambda k: -min(k, n_ao - k))
    for o in range(occupied):
        for k in order:
            move(o, k).start()

    entry = [jnp.int32(0)] * CAP
    filled = jnp.int32(0)
    for e in range(2 * count):
        hit = owners_ref[e % count, e // count] == me
        for c in range(CAP):
            entry[c] = jnp.where(jnp.logical_and(hit, filled == c), e, entry[c])
        filled = filled + hit.astype(jnp.int32)

    for o in range(occupied):
        own[o].wait()
        for k in order:
            move(o, k).wait_recv()

        def one_pair(p, carry, o=o):
            left = bufs[o][pairs_ref[p, 0]]
            right = bufs[o][pairs_ref[p, 1]]
            tile = lax.dot_general(
                left, right, (((0,), (0,)), ((), ())), preferred_element_type=jnp.float32
            )
            at = pl.ds(pl.multiple_of(p * block, block), block)
            if o == 0:
                acc[at] = tile
            else:
                acc[at] += tile
            return carry

        lax.fori_loop(0, count, one_pair, 0)

    swap = pltpu.make_async_remote_copy(
        src_ref=acc.at[pl.ds(pl.multiple_of(other * share, share), share)],
        dst_ref=from_core,
        send_sem=core_sem.at[0],
        recv_sem=core_sem.at[1],
        device_id={"aux": other},
        device_id_type=MESH,
    )
    swap.start()
    swap.wait()
    from_core[...] += acc[pl.ds(pl.multiple_of(core * share, share), share)]

    def part(k):
        return pltpu.make_async_remote_copy(
            src_ref=from_core.at[pl.ds(pl.multiple_of(peer(k) * size, size), size)],
            dst_ref=from_ao.at[me],
            send_sem=part_sem.at[0, k],
            recv_sem=part_sem.at[1, k],
            device_id={"ao": peer(k)},
            device_id_type=MESH,
        )

    for k in order:
        part(k).start()
    total = from_core[pl.ds(pl.multiple_of(me * size, size), size)]
    for k in order[::-1]:
        part(k).wait_recv()
        total = total + from_ao[source(k)]
    piece[...] = total

    def place(which_core, index):
        flat = which_core * n_ao + index
        return tiles.at[flat // pieces, lax.rem(flat, pieces)]

    def spread(k):
        return pltpu.make_async_remote_copy(
            src_ref=piece,
            dst_ref=place(core, me),
            send_sem=spread_sem.at[0, k],
            recv_sem=spread_sem.at[1, k],
            device_id={"ao": peer(k)},
            device_id_type=MESH,
        )

    def passed(k):
        return pltpu.make_async_remote_copy(
            src_ref=piece if k == 0 else place(core, source(k)),
            dst_ref=place(core, source(k)),
            send_sem=pass_sem.at[0, k],
            recv_sem=pass_sem.at[1, k],
            device_id={"aux": other},
            device_id_type=MESH,
        )

    for k in order:
        spread(k).start()
    passed(0).start()
    place(core, me)[...] = total
    for k in order[::-1]:
        spread(k).wait_recv()
        passed(k).start()
    for k in range(n_ao):
        passed(k).wait()

    for c in range(CAP):
        e = entry[c]
        mirrored = e >= count
        p = jnp.where(mirrored, e - count, e)
        tile = tiles[p].reshape(block, block)
        flipped = tile.T
        chosen = jnp.where(mirrored, flipped, tile)
        mine = jnp.where(core == 0, chosen[:half], chosen[half:])
        out_ref[c] = jnp.where(filled > c, mine, 0.0)

    for k in order:
        for o in range(occupied):
            move(o, k).wait_send()
        part(k).wait_send()
        spread(k).wait_send()


def on_device(factors, pairs, owners):
    n_ao = lax.axis_size("ao")
    n_aux = lax.axis_size("aux")
    occupied, local, block = factors.shape
    rows = local // n_ao
    count = pairs.shape[0]
    share = count * block // n_aux
    size = share // n_ao
    return pl.pallas_call(
        functools.partial(kernel, n_ao, n_aux, occupied),
        out_shape=jax.ShapeDtypeStruct((CAP, block // n_aux, block), jnp.float32),
        in_specs=[
            pl.BlockSpec(memory_space=pltpu.SMEM),
            pl.BlockSpec(memory_space=pltpu.SMEM),
            pl.BlockSpec(memory_space=pl.ANY),
        ],
        out_specs=pl.BlockSpec(memory_space=pltpu.VMEM),
        scratch_shapes=[pltpu.VMEM((n_ao, rows, block), jnp.bfloat16)] * occupied
        + [
            pltpu.VMEM((count * block, block), jnp.float32),
            pltpu.VMEM((share, block), jnp.float32),
            pltpu.VMEM((n_ao, size, block), jnp.float32),
            pltpu.VMEM((size, block), jnp.float32),
            pltpu.VMEM((count, block // size, size, block), jnp.float32),
            pltpu.SemaphoreType.DMA((occupied,)),
            pltpu.SemaphoreType.DMA((occupied, n_ao)),
            pltpu.SemaphoreType.DMA((occupied, n_ao)),
            pltpu.SemaphoreType.DMA((2,)),
            pltpu.SemaphoreType.DMA((2, n_ao)),
            pltpu.SemaphoreType.DMA((2, n_ao)),
            pltpu.SemaphoreType.DMA((2, n_ao)),
        ],
        compiler_params=pltpu.CompilerParams(
            collective_id=0, has_side_effects=True, vmem_limit_bytes=40 << 20
        ),
        cost_estimate=pl.CostEstimate(
            flops=2 * count * block * block * occupied * rows,
            bytes_accessed=factors.size * 2,
            transcendentals=0,
        ),
    )(pairs, owners, factors)


def solution(mesh):
    in_specs = (P(None, ("frag", "aux"), "ao"), P("frag", None), P("frag", None))
    out_specs = P(("frag", "ao"), "aux", None)
    return jax.shard_map(
        on_device, mesh=mesh, in_specs=in_specs, out_specs=out_specs, check_vma=False
    )
```

```python
import functools

import jax
import jax.numpy as jnp
from jax import lax
from jax.experimental import pallas as pl
from jax.experimental.pallas import tpu as pltpu
from jax.sharding import PartitionSpec as P

CAP = 4
MESH = pl.DeviceIdType.MESH


def chunks(occupied, rows):
    parts = [(o, 0, rows) for o in range(occupied - 1)]
    start = 0
    for size in (rows // 2, rows // 3, rows - rows // 2 - rows // 3):
        parts.append((occupied - 1, start, size))
        start += size
    return parts


def kernel(n_ao, n_aux, parts, pairs_hbm, owners_hbm, factors_ref, out_ref, *scratch):
    bufs = scratch[: len(parts)]
    scratch = scratch[len(parts) :]
    pairs_ref, owners_ref, acc, from_core, far, near, far_total, cross, piece, tiles = scratch[:10]
    table_sem, own_sem, send_sem, recv_sem, core_sem, far_sem, near_sem, cross_sem = scratch[10:18]
    spread_sem, relay_sem, pass_sem = scratch[18:]
    me = lax.axis_index("ao")
    core = lax.axis_index("aux")
    other = 1 - core
    block = out_ref.shape[2]
    rows = factors_ref.shape[1] // n_ao
    count = pairs_ref.shape[1]
    half = out_ref.shape[1]
    share = from_core.shape[0]
    size = share // n_ao
    pieces = block // size
    n_side = n_ao // 2
    first = me // n_side * n_side
    mirror = lax.rem(me + n_side, n_ao)

    def peer(k):
        return lax.rem(me + k, n_ao)

    def near_peer(k):
        return first + lax.rem(me - first + k, n_side)

    def near_source(k):
        return first + lax.rem(me - first + (n_side - k), n_side)

    def mirrored_of(index):
        return lax.rem(index + n_side, n_ao)

    barrier = pltpu.get_barrier_semaphore()
    for k in range(1, n_ao):
        pl.semaphore_signal(barrier, inc=1, device_id={"ao": peer(k)}, device_id_type=MESH)
    pl.semaphore_signal(barrier, inc=1, device_id={"aux": other}, device_id_type=MESH)
    tables = [
        pltpu.make_async_copy(pairs_hbm, pairs_ref, table_sem.at[0]),
        pltpu.make_async_copy(owners_hbm, owners_ref, table_sem.at[1]),
    ]
    own = []
    for i, (o, start, length) in enumerate(parts):
        own.append(
            pltpu.make_async_copy(
                factors_ref.at[o, pl.ds(pl.multiple_of(me * rows + start, 16), length)],
                bufs[i].at[me],
                own_sem.at[i],
            )
        )

    def move(i, k):
        o, start, length = parts[i]
        return pltpu.make_async_remote_copy(
            src_ref=factors_ref.at[o, pl.ds(pl.multiple_of(peer(k) * rows + start, 16), length)],
            dst_ref=bufs[i].at[me],
            send_sem=send_sem.at[i, k],
            recv_sem=recv_sem.at[i, k],
            device_id={"ao": peer(k)},
            device_id_type=MESH,
        )

    order = sorted(range(1, n_ao), key=lambda k: -min(k, n_ao - k))
    pl.semaphore_wait(barrier, n_ao)
    for i in range(len(parts)):
        for k in order:
            move(i, k).start()
    for copy in tables + own:
        copy.start()
    for copy in tables:
        copy.wait()

    entry = [jnp.int32(0)] * CAP
    filled = jnp.int32(0)
    for e in range(2 * count):
        hit = owners_ref[e // count, e % count] == me
        for c in range(CAP):
            entry[c] = jnp.where(jnp.logical_and(hit, filled == c), e, entry[c])
        filled = filled + hit.astype(jnp.int32)

    def tile_part(i, which_core):
        def one_pair(q, carry):
            p = which_core * (count // n_aux) + q
            left = bufs[i][pairs_ref[0, p]]
            right = bufs[i][pairs_ref[1, p]]
            tile = lax.dot_general(
                left, right, (((0,), (0,)), ((), ())), preferred_element_type=jnp.float32
            )
            at = pl.ds(pl.multiple_of(p * block, block), block)
            if i == 0:
                acc[at] = tile
            else:
                acc[at] += tile
            return carry

        lax.fori_loop(0, count // n_aux, one_pair, 0)

    swap = pltpu.make_async_remote_copy(
        src_ref=acc.at[pl.ds(pl.multiple_of(other * share, share), share)],
        dst_ref=from_core,
        send_sem=core_sem.at[0],
        recv_sem=core_sem.at[1],
        device_id={"aux": other},
        device_id_type=MESH,
    )
    for i in range(len(parts)):
        own[i].wait()
        for k in order:
            move(i, k).wait_recv()
        tile_part(i, other)
        if i == len(parts) - 1:
            swap.start()
        tile_part(i, core)
    swap.wait()
    from_core[...] += acc[pl.ds(pl.multiple_of(core * share, share), share)]

    def held(index):
        return from_core.at[pl.ds(pl.multiple_of(index * size, size), size)]

    def collect(k, distant):
        sem = far_sem if distant else near_sem
        return pltpu.make_async_remote_copy(
            src_ref=held(mirrored_of(near_peer(k)) if distant else near_peer(k)),
            dst_ref=(far if distant else near).at[k],
            send_sem=sem.at[0, k],
            recv_sem=sem.at[1, k],
            device_id={"ao": near_peer(k)},
            device_id_type=MESH,
        )

    for k in range(1, n_side):
        collect(k, True).start()
    for k in range(1, n_side):
        collect(k, False).start()
    total = held(mirror)[...]
    for k in range(1, n_side):
        collect(k, True).wait_recv()
        total = total + far[k]
    far_total[...] = total

    def across(src, dst, n):
        return pltpu.make_async_remote_copy(
            src_ref=src,
            dst_ref=dst,
            send_sem=cross_sem.at[0, n],
            recv_sem=cross_sem.at[1, n],
            device_id={"ao": mirror},
            device_id_type=MESH,
        )

    halves = across(far_total, cross, 0)
    halves.start()
    total = held(me)[...]
    for k in range(1, n_side):
        collect(k, False).wait_recv()
        total = total + near[k]
    halves.wait_recv()
    total = total + cross[...]
    piece[...] = total

    def place(which_core, index):
        flat = which_core * n_ao + index
        return tiles.at[flat // pieces, lax.rem(flat, pieces)]

    def spread(k, relayed):
        sem = relay_sem if relayed else spread_sem
        return pltpu.make_async_remote_copy(
            src_ref=place(core, mirror) if relayed else piece,
            dst_ref=place(core, mirror if relayed else me),
            send_sem=sem.at[0, k],
            recv_sem=sem.at[1, k],
            device_id={"ao": near_peer(k)},
            device_id_type=MESH,
        )

    def passed(n, index, src=None):
        return pltpu.make_async_remote_copy(
            src_ref=place(core, index) if src is None else src,
            dst_ref=place(core, index),
            send_sem=pass_sem.at[0, n],
            recv_sem=pass_sem.at[1, n],
            device_id={"aux": other},
            device_id_type=MESH,
        )

    swapped = across(piece, place(core, me), 1)
    swapped.start()
    for k in range(1, n_side):
        spread(k, False).start()
    passes = [passed(0, me, piece)]
    passes[-1].start()
    place(core, me)[...] = total
    swapped.wait_recv()
    for k in range(1, n_side):
        spread(k, True).start()
    passes.append(passed(n_side, mirror))
    passes[-1].start()
    for relayed in (False, True):
        for k in range(1, n_side):
            spread(k, relayed).wait_recv()
            index = near_source(k)
            passes.append(
                passed(k + n_side, mirrored_of(index)) if relayed else passed(k, index)
            )
            passes[-1].start()
    for copy in passes:
        copy.wait()

    for c in range(CAP):
        e = entry[c]
        mirrored = e >= count
        p = jnp.where(mirrored, e - count, e)
        tile = tiles[p].reshape(block, block)
        chosen = jnp.where(mirrored, tile.T, tile)
        mine = jnp.where(core == 0, chosen[:half], chosen[half:])
        out_ref[c] = jnp.where(filled > c, mine, 0.0)

    for i in range(len(parts)):
        for k in order:
            move(i, k).wait_send()
    for k in range(1, n_side):
        for second in (False, True):
            collect(k, second).wait_send()
            spread(k, second).wait_send()
    halves.wait_send()
    swapped.wait_send()


def on_device(factors, pairs, owners):
    n_ao = lax.axis_size("ao")
    n_aux = lax.axis_size("aux")
    occupied, local, block = factors.shape
    rows = local // n_ao
    count = pairs.shape[0]
    share = count * block // n_aux
    size = share // n_ao
    n_side = n_ao // 2
    parts = chunks(occupied, rows)
    dma = pltpu.SemaphoreType.DMA
    f32 = jnp.float32
    return pl.pallas_call(
        functools.partial(kernel, n_ao, n_aux, parts),
        out_shape=jax.ShapeDtypeStruct((CAP, block // n_aux, block), f32),
        in_specs=[pl.BlockSpec(memory_space=pl.ANY)] * 3,
        out_specs=pl.BlockSpec(memory_space=pltpu.VMEM),
        scratch_shapes=[
            pltpu.VMEM((n_ao, length, block), jnp.bfloat16) for _, _, length in parts
        ]
        + [
            pltpu.SMEM((2, count), jnp.int32),
            pltpu.SMEM((2, count), jnp.int32),
            pltpu.VMEM((count * block, block), f32),
            pltpu.VMEM((share, block), f32),
            pltpu.VMEM((n_side, size, block), f32),
            pltpu.VMEM((n_side, size, block), f32),
            pltpu.VMEM((size, block), f32),
            pltpu.VMEM((size, block), f32),
            pltpu.VMEM((size, block), f32),
            pltpu.VMEM((count, block // size, size, block), f32),
            dma((2,)),
            dma((len(parts),)),
            dma((len(parts), n_ao)),
            dma((len(parts), n_ao)),
            dma((2,)),
            dma((2, n_side)),
            dma((2, n_side)),
            dma((2, 2)),
            dma((2, n_side)),
            dma((2, n_side)),
            dma((2, n_ao)),
        ],
        compiler_params=pltpu.CompilerParams(
            collective_id=0, has_side_effects=True, vmem_limit_bytes=58 << 20
        ),
        cost_estimate=pl.CostEstimate(
            flops=2 * count * block * block * occupied * rows,
            bytes_accessed=factors.size * 2,
            transcendentals=0,
        ),
    )(pairs.T, owners.T, factors)


def solution(mesh):
    in_specs = (P(None, ("frag", "aux"), "ao"), P("frag", None), P("frag", None))
    out_specs = P(("frag", "ao"), "aux", None)
    return jax.shard_map(
        on_device, mesh=mesh, in_specs=in_specs, out_specs=out_specs, check_vma=False
    )
```

```python
import functools

import jax
import jax.numpy as jnp
from jax import lax
from jax.experimental import pallas as pl
from jax.experimental.pallas import tpu as pltpu
from jax.sharding import PartitionSpec as P

CAP = 4
MESH = pl.DeviceIdType.MESH


def chunks(occupied, rows):
    first = max(1, occupied - 1)
    parts = [(0, first, 0, rows)] + [(o, 1, 0, rows) for o in range(first, occupied - 1)]
    last = rows // 3
    return parts + [(occupied - 1, 1, 0, rows - last), (occupied - 1, 1, rows - last, last)]


def kernel(n_ao, n_aux, parts, pairs_hbm, owners_hbm, factors_ref, out_ref, *scratch):
    bufs = scratch[: len(parts)]
    scratch = scratch[len(parts) :]
    pairs_ref, owners_ref, acc, from_core, far, near, far_total, cross, piece, tiles = scratch[:10]
    table_sem, own_sem, send_sem, recv_sem, core_sem, far_sem, near_sem, cross_sem = scratch[10:18]
    spread_sem, relay_sem, pass_sem = scratch[18:]
    me = lax.axis_index("ao")
    core = lax.axis_index("aux")
    other = 1 - core
    block = out_ref.shape[2]
    rows = factors_ref.shape[1] // n_ao
    count = pairs_ref.shape[1]
    half = out_ref.shape[1]
    share = from_core.shape[0]
    size = share // n_ao
    pieces = block // size
    n_side = n_ao // 2
    first = me // n_side * n_side
    mirror = lax.rem(me + n_side, n_ao)

    def peer(k):
        return lax.rem(me + k, n_ao)

    def near_peer(k):
        return first + lax.rem(me - first + k, n_side)

    def near_source(k):
        return first + lax.rem(me - first + (n_side - k), n_side)

    def mirrored_of(index):
        return lax.rem(index + n_side, n_ao)

    barrier = pltpu.get_barrier_semaphore()
    for k in range(1, n_ao):
        pl.semaphore_signal(barrier, inc=1, device_id={"ao": peer(k)}, device_id_type=MESH)
    pl.semaphore_signal(barrier, inc=1, device_id={"aux": other}, device_id_type=MESH)
    tables = [
        pltpu.make_async_copy(pairs_hbm, pairs_ref, table_sem.at[0]),
        pltpu.make_async_copy(owners_hbm, owners_ref, table_sem.at[1]),
    ]
    own = []
    for i, (o, many, start, length) in enumerate(parts):
        own.append(
            pltpu.make_async_copy(
                factors_ref.at[
                    pl.ds(o, many), pl.ds(pl.multiple_of(me * rows + start, 16), length)
                ],
                bufs[i].at[me],
                own_sem.at[i],
            )
        )

    def move(i, k):
        o, many, start, length = parts[i]
        at = pl.ds(pl.multiple_of(peer(k) * rows + start, 16), length)
        return pltpu.make_async_remote_copy(
            src_ref=factors_ref.at[pl.ds(o, many), at],
            dst_ref=bufs[i].at[me],
            send_sem=send_sem.at[i, k],
            recv_sem=recv_sem.at[i, k],
            device_id={"ao": peer(k)},
            device_id_type=MESH,
        )

    order = sorted(range(1, n_ao), key=lambda k: -min(k, n_ao - k))
    pl.semaphore_wait(barrier, n_ao)
    for i in range(len(parts)):
        for k in order:
            move(i, k).start()
    for copy in tables + own:
        copy.start()
    for copy in tables:
        copy.wait()

    entry = [jnp.int32(0)] * CAP
    filled = jnp.int32(0)
    for e in range(2 * count):
        hit = owners_ref[e // count, e % count] == me
        for c in range(CAP):
            entry[c] = jnp.where(jnp.logical_and(hit, filled == c), e, entry[c])
        filled = filled + hit.astype(jnp.int32)

    def tile_part(i, which_core):
        def one_pair(q, carry):
            p = which_core * (count // n_aux) + q
            left = bufs[i][pairs_ref[0, p]].reshape(-1, block)
            right = bufs[i][pairs_ref[1, p]].reshape(-1, block)
            tile = lax.dot_general(
                left, right, (((0,), (0,)), ((), ())), preferred_element_type=jnp.float32
            )
            at = pl.ds(pl.multiple_of(p * block, block), block)
            if i == 0:
                acc[at] = tile
            else:
                acc[at] += tile
            return carry

        lax.fori_loop(0, count // n_aux, one_pair, 0, unroll=4)

    swap = pltpu.make_async_remote_copy(
        src_ref=acc.at[pl.ds(pl.multiple_of(other * share, share), share)],
        dst_ref=from_core,
        send_sem=core_sem.at[0],
        recv_sem=core_sem.at[1],
        device_id={"aux": other},
        device_id_type=MESH,
    )
    for i in range(len(parts)):
        own[i].wait()
        for k in order:
            move(i, k).wait_recv()
        tile_part(i, other)
        if i == len(parts) - 1:
            swap.start()
        tile_part(i, core)
    swap.wait()
    from_core[...] += acc[pl.ds(pl.multiple_of(core * share, share), share)]

    def held(index):
        return from_core.at[pl.ds(pl.multiple_of(index * size, size), size)]

    def collect(k, distant):
        sem = far_sem if distant else near_sem
        return pltpu.make_async_remote_copy(
            src_ref=held(mirrored_of(near_peer(k)) if distant else near_peer(k)),
            dst_ref=(far if distant else near).at[k],
            send_sem=sem.at[0, k],
            recv_sem=sem.at[1, k],
            device_id={"ao": near_peer(k)},
            device_id_type=MESH,
        )

    for k in range(1, n_side):
        collect(k, True).start()
    for k in range(1, n_side):
        collect(k, False).start()
    total = held(mirror)[...]
    for k in range(1, n_side):
        collect(k, True).wait_recv()
        total = total + far[k]
    far_total[...] = total

    def across(src, dst, n):
        return pltpu.make_async_remote_copy(
            src_ref=src,
            dst_ref=dst,
            send_sem=cross_sem.at[0, n],
            recv_sem=cross_sem.at[1, n],
            device_id={"ao": mirror},
            device_id_type=MESH,
        )

    halves = across(far_total, cross, 0)
    halves.start()
    total = held(me)[...]
    for k in range(1, n_side):
        collect(k, False).wait_recv()
        total = total + near[k]
    halves.wait_recv()
    total = total + cross[...]
    piece[...] = total

    def place(which_core, index):
        flat = which_core * n_ao + index
        return tiles.at[flat // pieces, lax.rem(flat, pieces)]

    def spread(k, relayed):
        sem = relay_sem if relayed else spread_sem
        return pltpu.make_async_remote_copy(
            src_ref=place(core, mirror) if relayed else piece,
            dst_ref=place(core, mirror if relayed else me),
            send_sem=sem.at[0, k],
            recv_sem=sem.at[1, k],
            device_id={"ao": near_peer(k)},
            device_id_type=MESH,
        )

    def passed(n, index, src=None):
        return pltpu.make_async_remote_copy(
            src_ref=place(core, index) if src is None else src,
            dst_ref=place(core, index),
            send_sem=pass_sem.at[0, n],
            recv_sem=pass_sem.at[1, n],
            device_id={"aux": other},
            device_id_type=MESH,
        )

    swapped = across(piece, place(core, me), 1)
    swapped.start()
    for k in range(1, n_side):
        spread(k, False).start()
    passes = [passed(0, me, piece)]
    passes[-1].start()
    place(core, me)[...] = total
    swapped.wait_recv()
    for k in range(1, n_side):
        spread(k, True).start()
    passes.append(passed(n_side, mirror))
    passes[-1].start()
    for relayed in (False, True):
        for k in range(1, n_side):
            spread(k, relayed).wait_recv()
            index = near_source(k)
            passes.append(
                passed(k + n_side, mirrored_of(index)) if relayed else passed(k, index)
            )
            passes[-1].start()
    for copy in passes:
        copy.wait()

    for c in range(CAP):
        e = entry[c]
        mirrored = e >= count
        p = jnp.where(mirrored, e - count, e)
        tile = tiles[p].reshape(block, block)
        chosen = jnp.where(mirrored, tile.T, tile)
        mine = jnp.where(core == 0, chosen[:half], chosen[half:])
        out_ref[c] = jnp.where(filled > c, mine, 0.0)

    for i in range(len(parts)):
        for k in order:
            move(i, k).wait_send()
    for k in range(1, n_side):
        for second in (False, True):
            collect(k, second).wait_send()
            spread(k, second).wait_send()
    halves.wait_send()
    swapped.wait_send()


def on_device(factors, pairs, owners):
    n_ao = lax.axis_size("ao")
    n_aux = lax.axis_size("aux")
    occupied, local, block = factors.shape
    rows = local // n_ao
    count = pairs.shape[0]
    share = count * block // n_aux
    size = share // n_ao
    n_side = n_ao // 2
    parts = chunks(occupied, rows)
    dma = pltpu.SemaphoreType.DMA
    f32 = jnp.float32
    return pl.pallas_call(
        functools.partial(kernel, n_ao, n_aux, parts),
        out_shape=jax.ShapeDtypeStruct((CAP, block // n_aux, block), f32),
        in_specs=[pl.BlockSpec(memory_space=pl.ANY)] * 3,
        out_specs=pl.BlockSpec(memory_space=pltpu.VMEM),
        scratch_shapes=[
            pltpu.VMEM((n_ao, many, length, block), jnp.bfloat16) for _, many, _, length in parts
        ]
        + [
            pltpu.SMEM((2, count), jnp.int32),
            pltpu.SMEM((2, count), jnp.int32),
            pltpu.VMEM((count * block, block), f32),
            pltpu.VMEM((share, block), f32),
            pltpu.VMEM((n_side, size, block), f32),
            pltpu.VMEM((n_side, size, block), f32),
            pltpu.VMEM((size, block), f32),
            pltpu.VMEM((size, block), f32),
            pltpu.VMEM((size, block), f32),
            pltpu.VMEM((count, block // size, size, block), f32),
            dma((2,)),
            dma((len(parts),)),
            dma((len(parts), n_ao)),
            dma((len(parts), n_ao)),
            dma((2,)),
            dma((2, n_side)),
            dma((2, n_side)),
            dma((2, 2)),
            dma((2, n_side)),
            dma((2, n_side)),
            dma((2, n_ao)),
        ],
        compiler_params=pltpu.CompilerParams(
            collective_id=0, has_side_effects=True, vmem_limit_bytes=57 << 20
        ),
        cost_estimate=pl.CostEstimate(
            flops=2 * count * block * block * occupied * rows,
            bytes_accessed=factors.size * 2,
            transcendentals=0,
        ),
    )(pairs.T, owners.T, factors)


def solution(mesh):
    in_specs = (P(None, ("frag", "aux"), "ao"), P("frag", None), P("frag", None))
    out_specs = P(("frag", "ao"), "aux", None)
    return jax.shard_map(
        on_device, mesh=mesh, in_specs=in_specs, out_specs=out_specs, check_vma=False
    )
```

```python
import functools

import jax
import jax.numpy as jnp
from jax import lax
from jax.experimental import pallas as pl
from jax.experimental.pallas import tpu as pltpu
from jax.sharding import PartitionSpec as P

CAP = 4
MESH = pl.DeviceIdType.MESH


def chunks(occupied, rows):
    first = max(1, occupied - 1)
    parts = [(0, first, 0, rows)] + [(o, 1, 0, rows) for o in range(first, occupied - 1)]
    last = rows // 3
    return parts + [(occupied - 1, 1, 0, rows - last), (occupied - 1, 1, rows - last, last)]


def kernel(n_ao, n_aux, parts, pairs_hbm, owners_hbm, factors_ref, out_ref, *scratch):
    bufs = scratch[: len(parts)]
    scratch = scratch[len(parts) :]
    pairs_ref, owners_ref, acc, from_core, far, near, far_total, cross, piece, tiles = scratch[:10]
    table_sem, own_sem, send_sem, recv_sem, core_sem, far_sem, near_sem, cross_sem = scratch[10:18]
    spread_sem, relay_sem, pass_sem = scratch[18:]
    me = lax.axis_index("ao")
    core = lax.axis_index("aux")
    other = 1 - core
    block = out_ref.shape[2]
    rows = factors_ref.shape[1] // n_ao
    count = pairs_ref.shape[1]
    half = out_ref.shape[1]
    share = from_core.shape[0]
    size = share // n_ao
    pieces = block // size
    n_side = n_ao // 2
    first = me // n_side * n_side
    mirror = lax.rem(me + n_side, n_ao)

    def peer(k):
        return lax.rem(me + k, n_ao)

    def near_peer(k):
        return first + lax.rem(me - first + k, n_side)

    def near_source(k):
        return first + lax.rem(me - first + (n_side - k), n_side)

    def mirrored_of(index):
        return lax.rem(index + n_side, n_ao)

    barrier = pltpu.get_barrier_semaphore()
    for k in range(1, n_ao):
        pl.semaphore_signal(barrier, inc=1, device_id={"ao": peer(k)}, device_id_type=MESH)
    pl.semaphore_signal(barrier, inc=1, device_id={"aux": other}, device_id_type=MESH)
    tables = [
        pltpu.make_async_copy(pairs_hbm, pairs_ref, table_sem.at[0]),
        pltpu.make_async_copy(owners_hbm, owners_ref, table_sem.at[1]),
    ]
    own = []
    for i, (o, many, start, length) in enumerate(parts):
        own.append(
            pltpu.make_async_copy(
                factors_ref.at[
                    pl.ds(o, many), pl.ds(pl.multiple_of(me * rows + start, 16), length)
                ],
                bufs[i].at[me],
                own_sem.at[i],
            )
        )

    def move(i, k):
        o, many, start, length = parts[i]
        at = pl.ds(pl.multiple_of(peer(k) * rows + start, 16), length)
        return pltpu.make_async_remote_copy(
            src_ref=factors_ref.at[pl.ds(o, many), at],
            dst_ref=bufs[i].at[me],
            send_sem=send_sem.at[i, k],
            recv_sem=recv_sem.at[i, k],
            device_id={"ao": peer(k)},
            device_id_type=MESH,
        )

    order = sorted(range(1, n_ao), key=lambda k: -min(k, n_ao - k))
    pl.semaphore_wait(barrier, n_ao)
    for i in range(len(parts)):
        for k in order:
            move(i, k).start()
    for copy in tables + own:
        copy.start()
    for copy in tables:
        copy.wait()

    entry = [jnp.int32(0)] * CAP
    filled = jnp.int32(0)
    for e in range(2 * count):
        hit = owners_ref[e // count, e % count] == me
        for c in range(CAP):
            entry[c] = jnp.where(jnp.logical_and(hit, filled == c), e, entry[c])
        filled = filled + hit.astype(jnp.int32)

    def tile_part(i, which_core):
        def one_pair(q, carry):
            p = which_core * (count // n_aux) + q
            left = bufs[i][pairs_ref[0, p]].reshape(-1, block)
            right = bufs[i][pairs_ref[1, p]].reshape(-1, block)
            tile = lax.dot_general(
                left, right, (((0,), (0,)), ((), ())), preferred_element_type=jnp.float32
            )
            at = pl.ds(pl.multiple_of(p * block, block), block)
            if i == 0:
                acc[at] = tile
            else:
                acc[at] += tile
            return carry

        lax.fori_loop(0, count // n_aux, one_pair, 0, unroll=4)

    swap = pltpu.make_async_remote_copy(
        src_ref=acc.at[pl.ds(pl.multiple_of(other * share, share), share)],
        dst_ref=from_core,
        send_sem=core_sem.at[0],
        recv_sem=core_sem.at[1],
        device_id={"aux": other},
        device_id_type=MESH,
    )
    for i in range(len(parts)):
        own[i].wait()
        for k in order:
            move(i, k).wait_recv()
        tile_part(i, other)
        if i == len(parts) - 1:
            swap.start()
        tile_part(i, core)
    swap.wait()
    from_core[...] += acc[pl.ds(pl.multiple_of(core * share, share), share)]

    def held(index):
        return from_core.at[pl.ds(pl.multiple_of(index * size, size), size)]

    def collect(k, distant):
        sem = far_sem if distant else near_sem
        return pltpu.make_async_remote_copy(
            src_ref=held(mirrored_of(near_peer(k)) if distant else near_peer(k)),
            dst_ref=(far if distant else near).at[k],
            send_sem=sem.at[0, k],
            recv_sem=sem.at[1, k],
            device_id={"ao": near_peer(k)},
            device_id_type=MESH,
        )

    for k in range(1, n_side):
        collect(k, True).start()
    for k in range(1, n_side):
        collect(k, False).start()
    total = held(mirror)[...]
    for k in range(1, n_side):
        collect(k, True).wait_recv()
        total = total + far[k]
    far_total[...] = total

    def across(src, dst, n):
        return pltpu.make_async_remote_copy(
            src_ref=src,
            dst_ref=dst,
            send_sem=cross_sem.at[0, n],
            recv_sem=cross_sem.at[1, n],
            device_id={"ao": mirror},
            device_id_type=MESH,
        )

    halves = across(far_total, cross, 0)
    halves.start()
    total = held(me)[...]
    for k in range(1, n_side):
        collect(k, False).wait_recv()
        total = total + near[k]
    halves.wait_recv()
    total = total + cross[...]
    piece[...] = total

    def place(which_core, index):
        flat = which_core * n_ao + index
        return tiles.at[flat // pieces, lax.rem(flat, pieces)]

    def spread(k, relayed):
        sem = relay_sem if relayed else spread_sem
        return pltpu.make_async_remote_copy(
            src_ref=place(core, mirror) if relayed else piece,
            dst_ref=place(core, mirror if relayed else me),
            send_sem=sem.at[0, k],
            recv_sem=sem.at[1, k],
            device_id={"ao": near_peer(k)},
            device_id_type=MESH,
        )

    def passed(n, index, src=None):
        return pltpu.make_async_remote_copy(
            src_ref=place(core, index) if src is None else src,
            dst_ref=place(core, index),
            send_sem=pass_sem.at[0, n],
            recv_sem=pass_sem.at[1, n],
            device_id={"aux": other},
            device_id_type=MESH,
        )

    swapped = across(piece, place(core, me), 1)
    swapped.start()
    for k in range(1, n_side):
        spread(k, False).start()
    passes = [passed(0, me, piece)]
    passes[-1].start()
    place(core, me)[...] = total
    swapped.wait_recv()
    for k in range(1, n_side):
        spread(k, True).start()
    passes.append(passed(n_side, mirror))
    passes[-1].start()
    for relayed in (False, True):
        for k in range(1, n_side):
            spread(k, relayed).wait_recv()
            index = near_source(k)
            passes.append(
                passed(k + n_side, mirrored_of(index)) if relayed else passed(k, index)
            )
            passes[-1].start()
    for copy in passes:
        copy.wait()

    for c in range(CAP):
        e = entry[c]
        mirrored = e >= count
        p = jnp.where(mirrored, e - count, e)
        tile = tiles[p].reshape(block, block)
        chosen = jnp.where(mirrored, tile.T, tile)
        mine = jnp.where(core == 0, chosen[:half], chosen[half:])
        out_ref[c] = jnp.where(filled > c, mine, 0.0)

    for i in range(len(parts)):
        for k in order:
            move(i, k).wait_send()
    for k in range(1, n_side):
        for second in (False, True):
            collect(k, second).wait_send()
            spread(k, second).wait_send()
    halves.wait_send()
    swapped.wait_send()


def on_device(factors, pairs, owners):
    n_ao = lax.axis_size("ao")
    n_aux = lax.axis_size("aux")
    occupied, local, block = factors.shape
    rows = local // n_ao
    count = pairs.shape[0]
    share = count * block // n_aux
    size = share // n_ao
    n_side = n_ao // 2
    parts = chunks(occupied, rows)
    dma = pltpu.SemaphoreType.DMA
    f32 = jnp.float32
    return pl.pallas_call(
        functools.partial(kernel, n_ao, n_aux, parts),
        out_shape=pltpu.VMEM((CAP, block // n_aux, block), f32),
        in_specs=[pl.BlockSpec(memory_space=pl.ANY)] * 3,
        out_specs=pl.BlockSpec(memory_space=pltpu.VMEM),
        scratch_shapes=[
            pltpu.VMEM((n_ao, many, length, block), jnp.bfloat16) for _, many, _, length in parts
        ]
        + [
            pltpu.SMEM((2, count), jnp.int32),
            pltpu.SMEM((2, count), jnp.int32),
            pltpu.VMEM((count * block, block), f32),
            pltpu.VMEM((share, block), f32),
            pltpu.VMEM((n_side, size, block), f32),
            pltpu.VMEM((n_side, size, block), f32),
            pltpu.VMEM((size, block), f32),
            pltpu.VMEM((size, block), f32),
            pltpu.VMEM((size, block), f32),
            pltpu.VMEM((count, block // size, size, block), f32),
            dma((2,)),
            dma((len(parts),)),
            dma((len(parts), n_ao)),
            dma((len(parts), n_ao)),
            dma((2,)),
            dma((2, n_side)),
            dma((2, n_side)),
            dma((2, 2)),
            dma((2, n_side)),
            dma((2, n_side)),
            dma((2, n_ao)),
        ],
        compiler_params=pltpu.CompilerParams(
            collective_id=0, has_side_effects=True, vmem_limit_bytes=57 << 20
        ),
        cost_estimate=pl.CostEstimate(
            flops=2 * count * block * block * occupied * rows,
            bytes_accessed=factors.size * 2,
            transcendentals=0,
        ),
    )(pairs.T, owners.T, factors)


def solution(mesh):
    in_specs = (P(None, ("frag", "aux"), "ao"), P("frag", None), P("frag", None))
    out_specs = P(("frag", "ao"), "aux", None)
    return jax.shard_map(
        on_device, mesh=mesh, in_specs=in_specs, out_specs=out_specs, check_vma=False
    )
```

```python
import functools

import jax
import jax.numpy as jnp
from jax import lax
from jax.experimental import pallas as pl
from jax.experimental.pallas import tpu as pltpu
from jax.sharding import PartitionSpec as P

CAP = 4
MESH = pl.DeviceIdType.MESH


def chunks(occupied, rows):
    first = max(1, occupied - 1)
    parts = [(0, first, 0, rows)] + [(o, 1, 0, rows) for o in range(first, occupied - 1)]
    last = rows // 6
    return parts + [(occupied - 1, 1, 0, rows - last), (occupied - 1, 1, rows - last, last)]


def kernel(n_ao, n_aux, parts, pairs_hbm, owners_hbm, factors_ref, out_ref, *scratch):
    bufs = scratch[: len(parts)]
    scratch = scratch[len(parts) :]
    pairs_ref, owners_ref, acc, from_core, far, near, far_total, cross, piece, tiles = scratch[:10]
    table_sem, own_sem, send_sem, recv_sem, core_sem, far_sem, near_sem, cross_sem = scratch[10:18]
    spread_sem, relay_sem, pass_sem = scratch[18:]
    me = lax.axis_index("ao")
    core = lax.axis_index("aux")
    other = 1 - core
    block = out_ref.shape[2]
    rows = factors_ref.shape[1] // n_ao
    count = pairs_ref.shape[1]
    half = out_ref.shape[1]
    share = from_core.shape[0]
    size = share // n_ao
    pieces = block // size
    n_side = n_ao // 2
    first = me // n_side * n_side
    mirror = lax.rem(me + n_side, n_ao)

    def peer(k):
        return lax.rem(me + k, n_ao)

    def near_peer(k):
        return first + lax.rem(me - first + k, n_side)

    def near_source(k):
        return first + lax.rem(me - first + (n_side - k), n_side)

    def mirrored_of(index):
        return lax.rem(index + n_side, n_ao)

    barrier = pltpu.get_barrier_semaphore()
    for k in range(1, n_ao):
        pl.semaphore_signal(barrier, inc=1, device_id={"ao": peer(k)}, device_id_type=MESH)
    pl.semaphore_signal(barrier, inc=1, device_id={"aux": other}, device_id_type=MESH)
    tables = [
        pltpu.make_async_copy(pairs_hbm, pairs_ref, table_sem.at[0]),
        pltpu.make_async_copy(owners_hbm, owners_ref, table_sem.at[1]),
    ]
    own = []
    for i, (o, many, start, length) in enumerate(parts):
        own.append(
            pltpu.make_async_copy(
                factors_ref.at[
                    pl.ds(o, many), pl.ds(pl.multiple_of(me * rows + start, 16), length)
                ],
                bufs[i].at[me],
                own_sem.at[i],
            )
        )

    def move(i, k):
        o, many, start, length = parts[i]
        at = pl.ds(pl.multiple_of(peer(k) * rows + start, 16), length)
        return pltpu.make_async_remote_copy(
            src_ref=factors_ref.at[pl.ds(o, many), at],
            dst_ref=bufs[i].at[me],
            send_sem=send_sem.at[i, k],
            recv_sem=recv_sem.at[i, k],
            device_id={"ao": peer(k)},
            device_id_type=MESH,
        )

    order = sorted(range(1, n_ao), key=lambda k: -min(k, n_ao - k))
    pl.semaphore_wait(barrier, n_ao)
    for i in range(len(parts)):
        for k in order:
            move(i, k).start()
    for copy in tables + own:
        copy.start()
    for copy in tables:
        copy.wait()

    entry = [jnp.int32(0)] * CAP
    filled = jnp.int32(0)
    for e in range(2 * count):
        hit = owners_ref[e // count, e % count] == me
        for c in range(CAP):
            entry[c] = jnp.where(jnp.logical_and(hit, filled == c), e, entry[c])
        filled = filled + hit.astype(jnp.int32)

    def tile_part(i, which_core):
        def one_pair(q, carry):
            p = which_core * (count // n_aux) + q
            left = bufs[i][pairs_ref[0, p]].reshape(-1, block)
            right = bufs[i][pairs_ref[1, p]].reshape(-1, block)
            tile = lax.dot_general(
                left, right, (((0,), (0,)), ((), ())), preferred_element_type=jnp.float32
            )
            at = pl.ds(pl.multiple_of(p * block, block), block)
            if i == 0:
                acc[at] = tile
            else:
                acc[at] += tile
            return carry

        lax.fori_loop(0, count // n_aux, one_pair, 0, unroll=4)

    swap = pltpu.make_async_remote_copy(
        src_ref=acc.at[pl.ds(pl.multiple_of(other * share, share), share)],
        dst_ref=from_core,
        send_sem=core_sem.at[0],
        recv_sem=core_sem.at[1],
        device_id={"aux": other},
        device_id_type=MESH,
    )
    for i in range(len(parts)):
        own[i].wait()
        for k in order:
            move(i, k).wait_recv()
        tile_part(i, other)
        if i == len(parts) - 1:
            swap.start()
        tile_part(i, core)
    swap.wait()

    def add_own(index):
        wide = n_side * size
        at = pl.ds(pl.multiple_of(index * size, wide), wide)
        from_core[at] += acc[pl.ds(pl.multiple_of(core * share + index * size, wide), wide)]

    add_own(n_side - first)

    def held(index):
        return from_core.at[pl.ds(pl.multiple_of(index * size, size), size)]

    def collect(k, distant):
        sem = far_sem if distant else near_sem
        return pltpu.make_async_remote_copy(
            src_ref=held(mirrored_of(near_peer(k)) if distant else near_peer(k)),
            dst_ref=(far if distant else near).at[k],
            send_sem=sem.at[0, k],
            recv_sem=sem.at[1, k],
            device_id={"ao": near_peer(k)},
            device_id_type=MESH,
        )

    for k in range(1, n_side):
        collect(k, True).start()
    add_own(first)
    for k in range(1, n_side):
        collect(k, False).start()
    total = held(mirror)[...]
    for k in range(1, n_side):
        collect(k, True).wait_recv()
        total = total + far[k]
    far_total[...] = total

    def across(src, dst, n):
        return pltpu.make_async_remote_copy(
            src_ref=src,
            dst_ref=dst,
            send_sem=cross_sem.at[0, n],
            recv_sem=cross_sem.at[1, n],
            device_id={"ao": mirror},
            device_id_type=MESH,
        )

    halves = across(far_total, cross, 0)
    halves.start()
    total = held(me)[...]
    for k in range(1, n_side):
        collect(k, False).wait_recv()
        total = total + near[k]
    halves.wait_recv()
    total = total + cross[...]
    piece[...] = total

    def place(which_core, index):
        flat = which_core * n_ao + index
        return tiles.at[flat // pieces, lax.rem(flat, pieces)]

    def spread(k, relayed):
        sem = relay_sem if relayed else spread_sem
        return pltpu.make_async_remote_copy(
            src_ref=place(core, mirror) if relayed else piece,
            dst_ref=place(core, mirror if relayed else me),
            send_sem=sem.at[0, k],
            recv_sem=sem.at[1, k],
            device_id={"ao": near_peer(k)},
            device_id_type=MESH,
        )

    def passed(n, index, src=None):
        return pltpu.make_async_remote_copy(
            src_ref=place(core, index) if src is None else src,
            dst_ref=place(core, index),
            send_sem=pass_sem.at[0, n],
            recv_sem=pass_sem.at[1, n],
            device_id={"aux": other},
            device_id_type=MESH,
        )

    swapped = across(piece, place(core, me), 1)
    swapped.start()
    for k in range(1, n_side):
        spread(k, False).start()
    passes = [passed(0, me, piece)]
    passes[-1].start()
    place(core, me)[...] = total
    swapped.wait_recv()
    for k in range(1, n_side):
        spread(k, True).start()
    passes.append(passed(n_side, mirror))
    passes[-1].start()
    for relayed in (False, True):
        for k in range(1, n_side):
            spread(k, relayed).wait_recv()
            index = near_source(k)
            passes.append(
                passed(k + n_side, mirrored_of(index)) if relayed else passed(k, index)
            )
            passes[-1].start()
    for copy in passes:
        copy.wait()

    for c in range(CAP):
        e = entry[c]
        mirrored = e >= count
        p = jnp.where(mirrored, e - count, e)
        tile = tiles[p].reshape(block, block)
        chosen = jnp.where(mirrored, tile.T, tile)
        mine = jnp.where(core == 0, chosen[:half], chosen[half:])
        out_ref[c] = jnp.where(filled > c, mine, 0.0)

    for i in range(len(parts)):
        for k in order:
            move(i, k).wait_send()
    for k in range(1, n_side):
        for second in (False, True):
            collect(k, second).wait_send()
            spread(k, second).wait_send()
    halves.wait_send()
    swapped.wait_send()


def on_device(factors, pairs, owners):
    n_ao = lax.axis_size("ao")
    n_aux = lax.axis_size("aux")
    occupied, local, block = factors.shape
    rows = local // n_ao
    count = pairs.shape[0]
    share = count * block // n_aux
    size = share // n_ao
    n_side = n_ao // 2
    parts = chunks(occupied, rows)
    dma = pltpu.SemaphoreType.DMA
    f32 = jnp.float32
    return pl.pallas_call(
        functools.partial(kernel, n_ao, n_aux, parts),
        out_shape=pltpu.VMEM((CAP, block // n_aux, block), f32),
        in_specs=[pl.BlockSpec(memory_space=pl.ANY)] * 3,
        out_specs=pl.BlockSpec(memory_space=pltpu.VMEM),
        scratch_shapes=[
            pltpu.VMEM((n_ao, many, length, block), jnp.bfloat16) for _, many, _, length in parts
        ]
        + [
            pltpu.SMEM((2, count), jnp.int32),
            pltpu.SMEM((2, count), jnp.int32),
            pltpu.VMEM((count * block, block), f32),
            pltpu.VMEM((share, block), f32),
            pltpu.VMEM((n_side, size, block), f32),
            pltpu.VMEM((n_side, size, block), f32),
            pltpu.VMEM((size, block), f32),
            pltpu.VMEM((size, block), f32),
            pltpu.VMEM((size, block), f32),
            pltpu.VMEM((count, block // size, size, block), f32),
            dma((2,)),
            dma((len(parts),)),
            dma((len(parts), n_ao)),
            dma((len(parts), n_ao)),
            dma((2,)),
            dma((2, n_side)),
            dma((2, n_side)),
            dma((2, 2)),
            dma((2, n_side)),
            dma((2, n_side)),
            dma((2, n_ao)),
        ],
        compiler_params=pltpu.CompilerParams(
            collective_id=0, has_side_effects=True, vmem_limit_bytes=57 << 20
        ),
        cost_estimate=pl.CostEstimate(
            flops=2 * count * block * block * occupied * rows,
            bytes_accessed=factors.size * 2,
            transcendentals=0,
        ),
    )(pairs.T, owners.T, factors)


def solution(mesh):
    in_specs = (P(None, ("frag", "aux"), "ao"), P("frag", None), P("frag", None))
    out_specs = P(("frag", "ao"), "aux", None)
    return jax.shard_map(
        on_device, mesh=mesh, in_specs=in_specs, out_specs=out_specs, check_vma=False
    )
```
